32 devices in a mesh: groups: 2 (over x), branch: 4 (over y, core), head: 4 (over z).
Axes of the slice: x: 2, y: 2, z: 4, core: 2. Of those that a mesh axis runs over, the one named last changes fastest.
Arguments:
- queries: bfloat16 [128, 8192], P(('groups', 'branch'), 'head'), parts along dimension 0, may hold values from -100 to 100, as said below
- root_keys: bfloat16 [32768, 1024], P(('groups', 'branch'), 'head'), parts along dimension 0, may hold values from -6 to 6
- root_values: bfloat16 [32768, 1024], P(('groups', 'branch'), 'head'), parts along dimension 0, may hold values from -6 to 6
- branch_keys: bfloat16 [8, 4096, 1024], P(('groups', 'branch'), None, 'head'), parts along dimension 0, may hold values from -6 to 6
- branch_values: bfloat16 [8, 4096, 1024], P(('groups', 'branch'), None, 'head'), parts along dimension 0, may hold values from -6 to 6
- branch_lengths: int32 [8], P(('groups', 'branch')), parts along dimension 0, may hold values from 512 to 4096, as said below
- row_branch: int32 [128], P('groups'), parts along dimension 0, may hold values from 0 to 3, as said below
Outputs:
- attended: bfloat16 [128, 8192], P(('groups', 'branch'), 'head'), parts along dimension 0
The draws below stay inside these ranges and needn't reach their ends.
There are 2 independent parts, one for each index of `groups`. The reference program is written for one: setup_inputs(seed, part) draws one part's arguments, and reference() takes and returns one part's arrays. A program takes and returns all parts, laid end to end along the dimension named above; each array names one. Nothing has to cross between parts.
Inputs may be any that keep to these rules, and one draw needn't show every extreme that they name: `queries`: query entries; rows may differ in scale. `row_branch`: no branch has more than 32 rows; some branch has exactly 32. `branch_lengths`: some branch has exactly 4096 live tokens.
All inputs are finite; a program needn't handle non-finite values.
Results may differ from the reference program's by a relative error of at most 0.006.
Values may be sent and summed in bfloat16 or wider, within the bound.
No kernel may reach another device: no remote copies, remote signals or barrier semaphores. Data moves between devices by JAX's collectives and lax.ppermute only.
A program may use at most 128 MiB of HBM per device.

```python
import jax
import jax.numpy as jnp
from jax import lax

QHEADS = 64
KVHEADS = 8
HD = 128
BMAX = 4096
BRANCHES = 4
ROWS = 64
MOST = 32
ROOT = 16384


def draw_queries(key, part):
    first = jax.random.fold_in(jax.random.fold_in(key, 5), 0)
    base = 3.0 * jax.random.normal(first, (ROWS, QHEADS * HD), jnp.float32)
    return jnp.clip(base, -15.0, 15.0).astype(jnp.bfloat16)


def draw_row_branch(key, part):
    first, second, third = jax.random.split(jax.random.fold_in(key, 11), 3)
    heavy = jax.random.randint(first, (), 0, BRANCHES)
    slots = jnp.arange((BRANCHES - 1) * MOST, dtype=jnp.int32) // MOST
    slots = slots + (slots >= heavy).astype(jnp.int32)
    chosen = jax.random.permutation(second, slots)[:ROWS - MOST]
    assigned = jnp.concatenate([jnp.full((MOST,), heavy, jnp.int32), chosen])
    return jax.random.permutation(third, assigned).astype(jnp.int32)


def draw_branch_lengths(key, part):
    first, second = jax.random.split(jax.random.fold_in(key, 23))
    lengths = jax.random.randint(first, (BRANCHES,), BMAX // 8, BMAX + 1)
    longest = jax.random.randint(second, (), 0, BRANCHES)
    return jnp.where(jnp.arange(BRANCHES) == longest, BMAX, lengths).astype(jnp.int32)


def steps_of(key, dims, cuts, least, top_value):
    gain = 1.0
    for position, shards_of in cuts:
        draws = jax.random.uniform(jax.random.fold_in(jax.random.fold_in(key, 6), position), (shards_of,), jnp.float32, least / len(cuts), top_value / len(cuts))
        gain = gain * jnp.repeat(jnp.exp(draws), dims[position] // shards_of).reshape((-1,) + (1,) * (len(dims) - 1 - position))
    return gain


def noise(stream_key, dims, spread, most, cuts=(), kind=jnp.bfloat16):
    level = steps_of(stream_key, dims, cuts, -0.22, 0.18) if cuts else 1.0
    values = jax.random.normal(stream_key, dims, jnp.float32) * spread * level
    return jnp.minimum(jnp.maximum(values, -most), most).astype(kind)


def setup_inputs(seed: int = 0, part: int = 0) -> dict:
    streams_of = jax.random.split(jax.random.key(seed), 8)
    part_keys = jax.random.split(jax.random.fold_in(streams_of[7], part), 8)
    queries = draw_queries(jax.random.fold_in(jax.random.fold_in(streams_of[7], part), 71), part)
    root_keys = noise(part_keys[1], (ROOT, KVHEADS * HD), 1.0, 6.0, ((0, 4), (1, 4)))
    root_values = noise(part_keys[2], (ROOT, KVHEADS * HD), 1.0, 6.0, ((0, 4), (1, 4)))
    branch_keys = noise(part_keys[3], (BRANCHES, BMAX, KVHEADS * HD), 1.0, 6.0, ((0, 4), (2, 4)))
    branch_values = noise(part_keys[4], (BRANCHES, BMAX, KVHEADS * HD), 1.0, 6.0, ((0, 4), (2, 4)))
    branch_lengths = draw_branch_lengths(jax.random.fold_in(jax.random.fold_in(streams_of[7], part), 71), part)
    row_branch = draw_row_branch(jax.random.fold_in(jax.random.fold_in(streams_of[7], part), 71), part)
    return {"queries": queries, "root_keys": root_keys, "root_values": root_values, "branch_keys": branch_keys, "branch_values": branch_values, "branch_lengths": branch_lengths, "row_branch": row_branch}


NEG = -1.0e30


def empty_part(count):
    return (jnp.full((count, QHEADS), NEG, jnp.float32), jnp.zeros((count, QHEADS), jnp.float32), jnp.zeros((count, QHEADS, HD), jnp.float32))


def combine(first, second):
    peak = jnp.maximum(first[0], second[0])
    scale_a = jnp.exp(first[0] - peak)
    scale_b = jnp.exp(second[0] - peak)
    return (peak, first[1] * scale_a + second[1] * scale_b, first[2] * scale_a[..., None] + second[2] * scale_b[..., None])


def partial_block(query, keys, values, valid):
    count = query.shape[0]
    scores = jnp.einsum("rgph,bgh->rgpb", query.astype(jnp.float32), keys.astype(jnp.float32)) * (HD ** -0.5)
    scores = jnp.where(valid, scores, NEG)
    peak = jnp.max(scores, axis=-1)
    weights = jnp.where(valid, jnp.exp(scores - peak[..., None]), 0.0)
    total = jnp.sum(weights, axis=-1)
    rounded = lax.optimization_barrier(weights.astype(jnp.bfloat16)).astype(jnp.float32)
    mixed = jnp.einsum("rgpb,bgh->rgph", rounded, values.astype(jnp.float32))
    return (peak.reshape(count, QHEADS), total.reshape(count, QHEADS), mixed.reshape(count, QHEADS, HD))


def reference(queries, root_keys, root_values, branch_keys, branch_values, branch_lengths, row_branch):
    per_group = QHEADS // KVHEADS
    query = queries.reshape(ROWS, KVHEADS, per_group, HD)
    block = min(512, ROOT)
    root_k = root_keys.reshape(ROOT // block, block, KVHEADS, HD)
    root_v = root_values.reshape(ROOT // block, block, KVHEADS, HD)

    def root_step(carry, pair):
        return combine(carry, partial_block(query, pair[0], pair[1], jnp.ones((block,), dtype=bool))), None

    root_part, _ = lax.scan(root_step, empty_part(ROWS), (root_k, root_v))
    inner = min(512, BMAX)
    slot_ids = jnp.arange(MOST, dtype=jnp.int32)
    positions = jnp.arange(BMAX, dtype=jnp.int32).reshape(BMAX // inner, inner)

    def branch_step(carry, index):
        member = row_branch == index
        ranking = jnp.cumsum(member.astype(jnp.int32)) - 1
        picker = member[None, :] & (ranking[None, :] == slot_ids[:, None])
        pick = picker.astype(jnp.float32)
        chosen = jnp.dot(pick, queries.astype(jnp.float32), precision=lax.Precision.HIGHEST).reshape(MOST, KVHEADS, per_group, HD)
        keys = lax.dynamic_index_in_dim(branch_keys, index, 0, keepdims=False).reshape(BMAX // inner, inner, KVHEADS, HD)
        values = lax.dynamic_index_in_dim(branch_values, index, 0, keepdims=False).reshape(BMAX // inner, inner, KVHEADS, HD)
        length = lax.dynamic_index_in_dim(branch_lengths, index, 0, keepdims=False)

        def key_step(state, triple):
            return combine(state, partial_block(chosen, triple[0], triple[1], triple[2] < length)), None

        part, _ = lax.scan(key_step, empty_part(MOST), (keys, values, positions))
        spread_peak = jnp.max(jnp.where(picker[:, :, None], part[0][:, None, :], NEG), axis=0)
        spread_total = jnp.einsum("sr,sk->rk", pick, part[1], precision=lax.Precision.HIGHEST)
        spread_mixed = jnp.einsum("sr,sk->rk", pick, part[2].reshape(MOST, QHEADS * HD), precision=lax.Precision.HIGHEST)
        return combine(carry, (spread_peak, spread_total, spread_mixed.reshape(ROWS, QHEADS, HD))), None

    branch_part, _ = lax.scan(branch_step, empty_part(ROWS), jnp.arange(BRANCHES, dtype=jnp.int32))
    peak, total, mixed = combine(root_part, branch_part)
    return (mixed / total[..., None]).reshape(ROWS, QHEADS * HD).astype(jnp.bfloat16)
```

```python
import functools

import jax
import jax.numpy as jnp
from jax import lax
from jax.experimental import pallas as pl
from jax.experimental.pallas import tpu as pltpu
from jax.sharding import PartitionSpec as P

QHEADS = 64
KVHEADS = 8
HD = 128
PER = QHEADS // KVHEADS
SCALE = HD**-0.5 * 1.4426950408889634
FEW = 16
LIMIT = 1e30
NEG = -1e30
F32 = jnp.float32
BF16 = jnp.bfloat16


def dot_nt(a, b):
    return lax.dot_general(a, b, (((1,), (1,)), ((), ())), preferred_element_type=F32)


def dot_nn(a, b):
    return lax.dot_general(a, b, (((1,), (0,)), ((), ())), preferred_element_type=F32)


def dot_tn(a, b):
    return lax.dot_general(a, b, (((0,), (0,)), ((), ())), preferred_element_type=F32)


def split3(x):
    high = x.astype(BF16)
    rest = x - high.astype(F32)
    mid = rest.astype(BF16)
    return high, mid, (rest - mid.astype(F32)).astype(BF16)


def stacked(query, group):
    return jnp.concatenate(
        [query[:, (group * PER + h) * HD : (group * PER + h + 1) * HD] for h in range(PER)], 0
    )


def add_block(query, mark, keys, values, live, acc):
    block = keys.shape[0]
    scores = dot_nt(keys, query)
    weights = jnp.exp2(scores * SCALE - mark * SCALE).astype(BF16)
    ones = jnp.ones((FEW, block), BF16)
    turned = values.T
    if live is not None:
        at = lax.broadcasted_iota(jnp.int32, (FEW, block), 1)
        ones = jnp.where(at < live, ones, jnp.zeros_like(ones))
        at = lax.broadcasted_iota(jnp.int32, (HD, block), 1)
        turned = jnp.where(at < live, turned, jnp.zeros_like(turned))
    acc[...] += dot_nn(jnp.concatenate([turned, ones], 0), weights)


def exact(query, keys_ref, values_ref, columns, length, acc, mark_ref):
    block = min(256, keys_ref.shape[0])
    mark_ref[...] = jnp.full(mark_ref.shape, NEG, F32)
    acc[...] = jnp.zeros(acc.shape, F32)

    @pl.loop(0, (length + block - 1) // block)
    def _(i):
        rows = pl.ds(pl.multiple_of(i * block, block), block)
        scores = dot_nt(keys_ref[rows, columns], query)
        valid = i * block + lax.broadcasted_iota(jnp.int32, scores.shape, 0) < length
        scores = jnp.where(valid, scores, NEG)
        old = mark_ref[...]
        new = jnp.maximum(old, jnp.max(scores, 0, keepdims=True))
        weights = jnp.where(valid, jnp.exp2((scores - new) * SCALE), 0.0)
        total = jnp.sum(weights, 0, keepdims=True)
        mixed = dot_tn(values_ref[rows, columns], weights.astype(BF16))
        more = jnp.concatenate([mixed, jnp.broadcast_to(total, (FEW, total.shape[1]))], 0)
        acc[...] = acc[...] * jnp.exp2((old - new) * SCALE) + more
        mark_ref[...] = new


def heads_last(rows, count):
    lines = [r[:, h * count : (h + 1) * count] for r in rows for h in range(PER)]
    lines.append(jnp.full((HD - len(lines), count), NEG, F32))
    return jnp.concatenate(lines, 0).T


def attend(
    pieces, axis, length_ref, owner_ref, *refs
):
    queries = refs[:pieces]
    root_k, root_v, branch_k, branch_v = refs[pieces : pieces + 4]
    outs = refs[pieces + 4 : 2 * pieces + 4]
    q_all, root_acc, root_mark, branch_acc, branch_mark = refs[2 * pieces + 4 :]
    local = queries[0].shape[0]
    rows = pieces * local
    slots = 2 * local
    width = queries[0].shape[1]
    groups = root_k.shape[1] // HD
    heads = groups * PER
    me = lax.axis_index(axis)
    length = length_ref[0]
    tokens = root_k.shape[0]

    for k in range(pieces):
        q_all[k * local : (k + 1) * local, :] = queries[k][...]

    row = lax.broadcasted_iota(jnp.int32, (rows, rows), 0)
    column = lax.broadcasted_iota(jnp.int32, (rows, rows), 1)
    moved = source_of(me, column // local, pieces) * local + lax.rem(column, local) == row
    owner = owner_ref[...].reshape(1, rows).astype(F32)
    owner = dot_nn(jnp.broadcast_to(owner, (8, rows)).astype(BF16), moved.astype(F32).astype(BF16))
    member = owner[:1] == me.astype(F32)
    before = dot_nn(
        jnp.broadcast_to(member.astype(F32), (8, rows)).astype(BF16),
        (row < column).astype(F32).astype(BF16),
    )[:1]
    slot = lax.broadcasted_iota(jnp.int32, (slots, rows), 0).astype(F32)
    picker = jnp.where(member & (before == slot), 1.0, 0.0).astype(BF16)
    chosen = dot_nn(picker, q_all[...]).astype(BF16)

    chunk = min(4 * local, rows)
    chunks = rows // chunk
    block = min(2048, tokens)

    def root(c, g):
        columns = slice(g * HD, (g + 1) * HD)
        query = stacked(q_all[pl.ds(pl.multiple_of(c * chunk, chunk), chunk), :], g)
        acc = root_acc.at[c, g]
        mark = jnp.max(dot_nt(root_k[:FEW, columns], query), 0, keepdims=True)
        root_mark[c, g] = mark
        acc[...] = jnp.zeros(acc.shape, F32)
        for i in range(tokens // block):
            part = slice(i * block, (i + 1) * block)
            add_block(query, mark, root_k[part, columns], root_v[part, columns], None, acc)

        @pl.when(jnp.logical_not(jnp.max(acc[HD : HD + 1, :]) < LIMIT))
        def _():
            exact(query, root_k, root_v, columns, tokens, acc, root_mark.at[c, g])

    def branch(g):
        columns = slice(g * HD, (g + 1) * HD)
        query = stacked(chosen, g)
        acc = branch_acc.at[g]
        mark = jnp.max(dot_nt(branch_k[:FEW, columns], query), 0, keepdims=True)
        branch_mark[g] = mark
        acc[...] = jnp.zeros(acc.shape, F32)
        size = min(1024, branch_k.shape[0])
        for i in range(branch_k.shape[0] // size):

            @pl.when(length > i * size)
            def _():
                part = slice(i * size, (i + 1) * size)
                add_block(
                    query, mark, branch_k[part, columns], branch_v[part, columns], length - i * size, acc
                )

        @pl.when(jnp.logical_not(jnp.max(acc[HD : HD + 1, :]) < LIMIT))
        def _():
            exact(query, branch_k, branch_v, columns, length, acc, branch_mark.at[g])

    if chunks == 1:
        for g in range(groups):
            root(0, g)
    else:

        @pl.loop(0, chunks)
        def _(c):
            for g in range(groups):
                root(c, g)

    for g in range(groups):
        branch(g)

    mixed_b = []
    for g in range(groups):
        turned = (branch_acc[g, :HD, :] / branch_acc[g, HD : HD + 1, :]).T
        mixed_b += [turned[h * slots : (h + 1) * slots] for h in range(PER)]
    mixed_b = jnp.concatenate(mixed_b, 1)
    level_b = heads_last(
        [branch_mark[g] * SCALE + jnp.log2(branch_acc[g, HD : HD + 1, :]) for g in range(groups)], slots
    )
    for c in range(chunks):
        there = slice(c * chunk, (c + 1) * chunk)
        pick = picker[:, there]
        high = mixed_b.astype(BF16)
        low = (mixed_b - high.astype(F32)).astype(BF16)
        spread = dot_tn(pick, high) + dot_tn(pick, low)
        first, second, third = split3(level_b)
        level = dot_tn(pick, first) + dot_tn(pick, second) + dot_tn(pick, third)
        held = jnp.sum(dot_tn(pick, jnp.ones((slots, HD), BF16)), 1, keepdims=True) > 0
        level = jnp.where(held, level, NEG)
        level_r = heads_last(
            [
                root_mark[c, g] * SCALE + jnp.log2(root_acc[c, g, HD : HD + 1, :])
                for g in range(groups)
            ],
            chunk,
        )
        top = jnp.maximum(level, level_r)
        weight_r = jnp.exp2(level_r - top)
        weight_b = jnp.exp2(level - top)
        total = weight_r + weight_b
        share_r = weight_r / total
        share_b = weight_b / total
        first, second, third = split3(top + jnp.log2(total))
        lanes = HD // 4
        aux = jnp.concatenate(
            [first[:, :lanes], second[:, :lanes], third[:, :lanes], first[:, :lanes]], 1
        )
        per_out = chunk // local
        for g in range(groups):
            turned = (root_acc[c, g, :HD, :] / root_acc[c, g, HD : HD + 1, :]).T
            for h in range(PER):
                head = g * PER + h
                tile = slice(head * HD, (head + 1) * HD)
                joined = (
                    turned[h * chunk : (h + 1) * chunk] * share_r[:, head : head + 1]
                    + spread[:, tile] * share_b[:, head : head + 1]
                ).astype(BF16)
                for j in range(per_out):
                    outs[c * per_out + j][:, tile] = joined[j * local : (j + 1) * local]
        for j in range(per_out):
            outs[c * per_out + j][:, width:] = aux[j * local : (j + 1) * local]


def join(pieces, *refs):
    parts, out = refs[:pieces], refs[pieces]
    width = out.shape[1]
    lanes = HD // 4
    levels = []
    for part in parts:
        aux = part[:, width:].astype(F32)
        levels.append(
            aux[:, :lanes] + aux[:, lanes : 2 * lanes] + aux[:, 2 * lanes : 3 * lanes]
        )
    top = functools.reduce(jnp.maximum, levels)
    weights = [jnp.exp2(level - top) for level in levels]
    total = functools.reduce(jnp.add, weights)
    shares = [weight / total for weight in weights]
    for head in range(width // HD):
        tile = slice(head * HD, (head + 1) * HD)
        out[:, tile] = functools.reduce(
            jnp.add,
            [
                part[:, tile].astype(F32) * share[:, head : head + 1]
                for part, share in zip(parts, shares)
            ],
        ).astype(BF16)


def source_of(me, step, count):
    if count & (count - 1) == 0:
        return me ^ step
    return lax.rem(me + step, count)


def pairs(step, count):
    return [(int(source_of_int(i, step, count)), i) for i in range(count)]


def source_of_int(me, step, count):
    return me ^ step if count & (count - 1) == 0 else (me + step) % count


def on_device(
    axis, count, queries, root_keys, root_values, branch_keys, branch_values, branch_lengths, row_branch
):
    local, width = queries.shape
    groups = root_keys.shape[1] // HD
    rows = count * local
    chunk = min(4 * local, rows)
    got = [queries] + [lax.ppermute(queries, axis, pairs(k, count)) for k in range(1, count)]
    vmem = pl.BlockSpec(memory_space=pltpu.VMEM)
    smem = pl.BlockSpec(memory_space=pltpu.SMEM)
    parts = pl.pallas_call(
        functools.partial(attend, count, axis),
        out_shape=[jax.ShapeDtypeStruct((local, width + HD), BF16)] * count,
        in_specs=[smem] + [vmem] * (count + 5),
        out_specs=[vmem] * count,
        scratch_shapes=[
            pltpu.VMEM((rows, width), BF16),
            pltpu.VMEM((rows // chunk, groups, HD + FEW, PER * chunk), F32),
            pltpu.VMEM((rows // chunk, groups, 1, PER * chunk), F32),
            pltpu.VMEM((groups, HD + FEW, PER * 2 * local), F32),
            pltpu.VMEM((groups, 1, PER * 2 * local), F32),
        ],
        compiler_params=pltpu.CompilerParams(vmem_limit_bytes=56 * 2**20),
        name="attend",
    )(
        branch_lengths,
        row_branch,
        *got,
        root_keys,
        root_values,
        branch_keys.reshape(branch_keys.shape[1:]),
        branch_values.reshape(branch_values.shape[1:]),
    )
    back = [parts[0]] + [
        lax.ppermute(parts[k], axis, [(b, a) for a, b in pairs(k, count)]) for k in range(1, count)
    ]
    return pl.pallas_call(
        functools.partial(join, count),
        out_shape=jax.ShapeDtypeStruct((local, width), BF16),
        in_specs=[vmem] * count,
        out_specs=vmem,
        name="join",
    )(*back)


def solution(mesh):
    placed = (
        P(("groups", "branch"), "head"),
        P(("groups", "branch"), "head"),
        P(("groups", "branch"), "head"),
        P(("groups", "branch"), None, "head"),
        P(("groups", "branch"), None, "head"),
        P(("groups", "branch")),
        P("groups"),
    )
    return jax.shard_map(
        functools.partial(on_device, "branch", mesh.shape["branch"]),
        mesh=mesh,
        in_specs=placed,
        out_specs=P(("groups", "branch"), "head"),
        check_vma=False,
    )
```

```python
import functools

import jax
import jax.numpy as jnp
from jax import lax
from jax.experimental import pallas as pl
from jax.experimental.pallas import tpu as pltpu
from jax.sharding import PartitionSpec as P

QHEADS = 64
KVHEADS = 8
HD = 128
PER = QHEADS // KVHEADS
SCALE = HD**-0.5 * 1.4426950408889634
FEW = 16
LIMIT = 1e30
NEG = -1e30
LANES = HD // 4
BLOCK = 2048
F32 = jnp.float32
BF16 = jnp.bfloat16


def dot_nt(a, b):
    return lax.dot_general(a, b, (((1,), (1,)), ((), ())), preferred_element_type=F32)


def dot_nn(a, b):
    return lax.dot_general(a, b, (((1,), (0,)), ((), ())), preferred_element_type=F32)


def dot_tn(a, b):
    return lax.dot_general(a, b, (((0,), (0,)), ((), ())), preferred_element_type=F32)


def split3(x):
    high = x.astype(BF16)
    rest = x - high.astype(F32)
    mid = rest.astype(BF16)
    return high, mid, (rest - mid.astype(F32)).astype(BF16)


def source_of(me, step, count):
    if count & (count - 1) == 0:
        return me ^ step
    return (me + step) % count


def stacked(query, group):
    first = group * PER
    return jnp.concatenate([query[:, h * HD : (h + 1) * HD] for h in range(first, first + PER)], 0)


def turned_values(values, live):
    ones = jnp.ones((FEW, values.shape[0]), BF16)
    both = jnp.concatenate([values.T, ones], 0)
    if live is None:
        return both
    at = lax.broadcasted_iota(jnp.int32, both.shape, 1)
    return jnp.where(at < live, both, jnp.zeros_like(both))


def of_group(keys_ref, turned_ref, group, there):
    wide = keys_ref.shape[1]
    columns = slice(group * HD, (group + 1) * HD)
    turned = jnp.concatenate([turned_ref[columns, there], turned_ref[wide:, there]], 0)
    return keys_ref[there, columns], turned


def weighted(keys_ref, turned_ref, group, there, query, mark):
    keys, turned = of_group(keys_ref, turned_ref, group, there)
    weights = jnp.exp2(dot_nt(keys, query) * SCALE - mark * SCALE)
    return dot_nn(turned, weights.astype(BF16))


def blocks(tokens):
    size = min(BLOCK, tokens)
    return [slice(i, i + size) for i in range(0, tokens, size)]


def attend(query, keys_ref, turned_ref, acc, marks, length=None):
    groups = acc.shape[0]
    queries = [stacked(query, g) for g in range(groups)]
    whole = blocks(keys_ref.shape[0])
    first = whole[:1] if length is not None else whole
    for g, q in enumerate(queries):
        mark = jnp.max(dot_nt(keys_ref[:FEW, g * HD : (g + 1) * HD], q), 0, keepdims=True)
        marks[g] = mark
        parts = [weighted(keys_ref, turned_ref, g, there, q, mark) for there in first]
        acc[g] = functools.reduce(jnp.add, parts)
    for there in whole[len(first) :]:

        @pl.when(length > there.start)
        def _():
            for g, q in enumerate(queries):
                acc[g] += weighted(keys_ref, turned_ref, g, there, q, marks[g])


def overflowed(acc):
    return jnp.max(jnp.where(acc[:, HD : HD + 1, :] < LIMIT, 0.0, 1.0)) > 0.0


def again(query, keys_ref, turned_ref, acc, marks, length):
    block = min(256, keys_ref.shape[0])
    for g in range(acc.shape[0]):
        q = stacked(query, g)
        marks[g] = jnp.full(marks.shape[1:], NEG, F32)
        acc[g] = jnp.zeros(acc.shape[1:], F32)

        @pl.loop(0, (length + block - 1) // block)
        def _(i):
            keys, turned = of_group(
                keys_ref, turned_ref, g, pl.ds(pl.multiple_of(i * block, block), block)
            )
            scores = dot_nt(keys, q)
            valid = i * block + lax.broadcasted_iota(jnp.int32, scores.shape, 0) < length
            scores = jnp.where(valid, scores, NEG)
            old = marks[g]
            new = jnp.maximum(old, jnp.max(scores, 0, keepdims=True))
            weights = jnp.where(valid, jnp.exp2((scores - new) * SCALE), 0.0)
            acc[g] = acc[g] * jnp.exp2((old - new) * SCALE) + dot_nn(turned, weights.astype(BF16))
            marks[g] = new


def finish(acc, marks):
    groups = acc.shape[0]
    rows = acc.shape[2] // PER
    tiles, lines = [], []
    for g in range(groups):
        total = acc[g, HD : HD + 1, :]
        mean = (acc[g, :HD, :] * (1.0 / total)).T
        tiles += [mean[h * rows : (h + 1) * rows] for h in range(PER)]
        level = marks[g] * SCALE + jnp.log2(total)
        lines += [level[:, h * rows : (h + 1) * rows] for h in range(PER)]
    lines.append(jnp.full((HD - len(lines), rows), NEG, F32))
    return tiles, jnp.concatenate(lines, 0).T


def joined(tiles, level, spread, level_b):
    top = jnp.maximum(level, level_b)
    weight = jnp.exp2(level - top)
    weight_b = jnp.exp2(level_b - top)
    total = weight + weight_b
    share = weight / total
    share_b = weight_b / total
    tiles = [
        mean * share[:, head : head + 1]
        + spread[:, head * HD : (head + 1) * HD] * share_b[:, head : head + 1]
        for head, mean in enumerate(tiles)
    ]
    return tiles, top + jnp.log2(total)


def pack(tiles, level, out):
    for head, mean in enumerate(tiles):
        out[:, head * HD : (head + 1) * HD] = mean.astype(BF16)
    parts = [p[:, :LANES] for p in split3(level)]
    out[:, len(tiles) * HD :] = jnp.concatenate(parts + parts[:1], 1)


def prepare(
    count, axis, length_ref, owner_hbm, query_hbm, root_k_hbm, root_v_hbm, branch_k_hbm, branch_v_hbm,
    root_k, root_t, branch_k, branch_t, query_ref, picker_ref, owner_ref, root_v, branch_v, sems,
):
    local = query_ref.shape[0]
    rows = count * local
    slots = 2 * local
    copies = []

    def fetch(source, target):
        copies.append(pltpu.make_async_copy(source, target, sems.at[len(copies)]))
        return copies[-1]

    small = [fetch(owner_hbm, owner_ref), fetch(query_hbm, query_ref)]
    values = []
    for source, target, turned in ((root_v_hbm, root_v, root_t), (branch_v_hbm, branch_v, branch_t)):
        for there in parts_of(source.shape[0]):
            copy = fetch(source.at[pl.ds(there.start, there.stop - there.start), :], target.at[there, :])
            values.append((copy, target, turned, there))
    keys = [fetch(root_k_hbm, root_k), fetch(branch_k_hbm, branch_k)]
    for copy in copies:
        copy.start()

    me = lax.axis_index(axis)
    row = lax.broadcasted_iota(jnp.int32, (rows, rows), 0)
    column = lax.broadcasted_iota(jnp.int32, (rows, rows), 1)
    moved = source_of(me, column // local, count) * local + column % local == row
    small[0].wait()
    owner = owner_ref[...].reshape(1, rows).astype(F32)
    owner = dot_nn(jnp.broadcast_to(owner, (8, rows)).astype(BF16), moved.astype(F32).astype(BF16))
    member = owner[:1] == me.astype(F32)
    before = dot_nn(
        jnp.broadcast_to(member.astype(F32), (8, rows)).astype(BF16),
        (row < column).astype(F32).astype(BF16),
    )[:1]
    slot = lax.broadcasted_iota(jnp.int32, (slots, rows), 0).astype(F32)
    picker_ref[...] = jnp.where(member & (before == slot), 1.0, 0.0).astype(BF16)

    length = length_ref[0]
    for copy, source, turned, there in values:
        copy.wait()
        live = length - there.start if turned is branch_t else None
        turned[:, there] = turned_values(source[there, :], live)
    for copy in (small[1], *keys):
        copy.wait()


def parts_of(tokens):
    size = min(1024, tokens)
    return [slice(i, i + size) for i in range(0, tokens, size)]


def unit(first, second, root_k, root_t, mean_ref, level_ref, acc, marks):
    query = jnp.concatenate([first[...], second[...]], 0)
    attend(query, root_k, root_t, acc, marks)

    @pl.when(overflowed(acc))
    def _():
        again(query, root_k, root_t, acc, marks, root_k.shape[0])

    tiles, level = finish(acc, marks)
    for head, mean in enumerate(tiles):
        mean_ref[:, head * HD : (head + 1) * HD] = mean
    level_ref[...] = level


def main(count, *refs):
    length_ref, picker_ref, root_k, root_t, branch_k, branch_t = refs[:6]
    refs = refs[6:]
    queries, refs = refs[:count], refs[count:]
    more = max(0, count // 2 - 2)
    means, refs = refs[:more], refs[more:]
    levels, refs = refs[:more], refs[more:]
    outs, refs = refs[: count - 2], refs[count - 2 :]
    spread_ref, level_ref, root_acc, root_marks, branch_acc, branch_marks = refs
    local = queries[0].shape[0]
    length = length_ref[0]
    picker = picker_ref[...]
    pieces = [q[...] for q in queries]
    query = jnp.concatenate(pieces[2:4], 0)
    chosen = dot_nn(picker, jnp.concatenate(pieces, 0)).astype(BF16)
    attend(query, root_k, root_t, root_acc, root_marks)
    attend(chosen, branch_k, branch_t, branch_acc, branch_marks, length)

    @pl.when(overflowed(root_acc) | overflowed(branch_acc))
    def _():
        again(query, root_k, root_t, root_acc, root_marks, root_k.shape[0])
        again(chosen, branch_k, branch_t, branch_acc, branch_marks, length)

    tiles, level = finish(branch_acc, branch_marks)
    mixed = jnp.concatenate(tiles, 1)
    high = mixed.astype(BF16)
    low = (mixed - high.astype(F32)).astype(BF16)
    parts = split3(level)
    spread = dot_tn(picker, high) + dot_tn(picker, low)
    level_b = functools.reduce(jnp.add, [dot_tn(picker, part) for part in parts])
    held = dot_tn(picker, jnp.ones((2 * local, HD), BF16)) > 0.0
    level_b = jnp.where(held, level_b, NEG)
    spread_ref[...] = spread[: 2 * local]
    level_ref[...] = level_b[: 2 * local]
    for pair in range(1, count // 2):
        if pair == 1:
            tiles, level = finish(root_acc, root_marks)
        else:
            mean = means[pair - 2][...]
            tiles = [mean[:, i : i + HD] for i in range(0, mean.shape[1], HD)]
            level = levels[pair - 2][...]
        there = slice(2 * pair * local, 2 * (pair + 1) * local)
        tiles, level = joined(tiles, level, spread[there], level_b[there])
        for j in range(2):
            mine = slice(j * local, (j + 1) * local)
            pack([t[mine] for t in tiles], level[mine], outs[2 * (pair - 1) + j])


def local_pair(first, second, root_k, root_t, spread, level_b, mean_ref, level_ref, out, acc, marks):
    local = first.shape[0]
    query = jnp.concatenate([first[...], second[...]], 0)
    attend(query, root_k, root_t, acc, marks)

    @pl.when(overflowed(acc))
    def _():
        again(query, root_k, root_t, acc, marks, root_k.shape[0])

    tiles, level = finish(acc, marks)
    tiles, level = joined(tiles, level, spread[...], level_b[...])
    pack([t[local:] for t in tiles], level[local:], out)
    for head, mean in enumerate(tiles):
        mean_ref[:, head * HD : (head + 1) * HD] = mean[:local]
    level_ref[...] = level[:local]


def join(*refs):
    mean, level, out = refs[-3:]
    parts = refs[:-3]
    width = out.shape[1]
    levels = [level[:, :LANES]]
    for part in parts:
        aux = part[:, width:].astype(F32)
        levels.append(aux[:, :LANES] + aux[:, LANES : 2 * LANES] + aux[:, 2 * LANES : 3 * LANES])
    top = functools.reduce(jnp.maximum, levels)
    weights = [jnp.exp2(level - top) for level in levels]
    over = 1.0 / functools.reduce(jnp.add, weights)
    shares = [weight * over for weight in weights]
    for head in range(width // HD):
        tile = slice(head * HD, (head + 1) * HD)
        terms = [
            part[:, tile].astype(F32) * share[:, head : head + 1]
            for part, share in zip((mean, *parts), shares)
        ]
        out[:, tile] = functools.reduce(jnp.add, terms).astype(BF16)


def near(x):
    return pltpu.with_memory_space_constraint(x, pltpu.VMEM)


def call(kernel, name, outs, scratch, operands, smem=0, far=0, room=24, cost=None):
    vmem = pl.BlockSpec(memory_space=pltpu.VMEM)
    return pl.pallas_call(
        kernel,
        out_shape=[pltpu.VMEM(shape, dtype) for shape, dtype in outs],
        in_specs=[pl.BlockSpec(memory_space=pltpu.SMEM)] * smem
        + [pl.BlockSpec(memory_space=pltpu.HBM)] * far
        + [vmem] * (len(operands) - smem - far),
        out_specs=[vmem] * len(outs),
        scratch_shapes=scratch,
        compiler_params=pltpu.CompilerParams(vmem_limit_bytes=room * 2**20),
        cost_estimate=cost,
        name=name,
    )(
        *operands[:smem],
        *[pltpu.with_memory_space_constraint(x, pltpu.HBM) for x in operands[smem : smem + far]],
        *map(near, operands[smem + far :]),
    )


def on_device(
    axis, count, queries, root_keys, root_values, branch_keys, branch_values, branch_lengths, row_branch
):
    local, width = queries.shape
    tokens, wide = root_keys.shape
    kept = branch_keys.shape[1]
    pair = 2 * local
    columns = pair * PER
    sums = [
        pltpu.VMEM((wide // HD, HD + FEW, columns), F32),
        pltpu.VMEM((wide // HD, 1, columns), F32),
    ]
    message = ((local, width + HD), BF16)
    pair_form = [((pair, width), F32), ((pair, HD), F32)]

    def moved(x, step, back=False):
        pairs = [(source_of(i, step, count), i) for i in range(count)]
        return lax.ppermute(x, axis, [(b, a) for a, b in pairs] if back else pairs)

    got = {k: moved(queries, k) for k in [*range(2, count), 1]}
    root_k, root_t, branch_k, branch_t, own, picker = call(
        functools.partial(prepare, count, axis),
        "prepare",
        [
            ((tokens, wide), BF16),
            ((wide + FEW, tokens), BF16),
            ((kept, wide), BF16),
            ((wide + FEW, kept), BF16),
            ((local, width), BF16),
            ((pair, count * local), BF16),
        ],
        [
            pltpu.VMEM((count * local,), jnp.int32),
            pltpu.VMEM((tokens, wide), BF16),
            pltpu.VMEM((kept, wide), BF16),
            pltpu.SemaphoreType.DMA((4 + len(parts_of(tokens)) + len(parts_of(kept)),)),
        ],
        [
            branch_lengths,
            row_branch,
            queries,
            root_keys,
            root_values,
            branch_keys.reshape(branch_keys.shape[1:]),
            branch_values.reshape(branch_values.shape[1:]),
        ],
        smem=1,
        far=6,
    )
    got[0] = own
    units = [
        call(unit, "unit", pair_form, sums, [got[k], got[k + 1], root_k, root_t])
        for k in range(4, count, 2)
    ]
    *outs, spread, level_b = call(
        functools.partial(main, count),
        "main",
        [message] * (count - 2) + pair_form,
        sums + sums,
        [branch_lengths, picker, root_k, root_t, branch_k, branch_t]
        + [got[k] for k in range(count)]
        + [u[0] for u in units]
        + [u[1] for u in units],
        smem=1,
    )
    arrived = [moved(out, k, back=True) for k, out in enumerate(outs, 2)]
    mean, level, out = call(
        local_pair,
        "local_pair",
        [((local, width), F32), ((local, HD), F32), message],
        sums,
        [got[0], got[1], root_k, root_t, spread, level_b],
        cost=pl.CostEstimate(
            flops=4 * pair * tokens * width,
            transcendentals=pair * tokens * width // HD,
            bytes_accessed=4 * tokens * wide,
        ),
    )
    arrived.append(moved(out, 1, back=True))
    vmem = pl.BlockSpec(memory_space=pltpu.VMEM)
    return pl.pallas_call(
        join,
        out_shape=jax.ShapeDtypeStruct((local, width), BF16),
        in_specs=[vmem] * (1 + count),
        out_specs=vmem,
        compiler_params=pltpu.CompilerParams(vmem_limit_bytes=8 * 2**20),
        name="join",
    )(*map(near, [*arrived, mean, level]))


def solution(mesh):
    placed = (
        P(("groups", "branch"), "head"),
        P(("groups", "branch"), "head"),
        P(("groups", "branch"), "head"),
        P(("groups", "branch"), None, "head"),
        P(("groups", "branch"), None, "head"),
        P(("groups", "branch")),
        P("groups"),
    )
    return jax.shard_map(
        functools.partial(on_device, "branch", mesh.shape["branch"]),
        mesh=mesh,
        in_specs=placed,
        out_specs=P(("groups", "branch"), "head"),
        check_vma=False,
    )
```

```python
import functools

import jax
import jax.numpy as jnp
from jax import lax
from jax.experimental import pallas as pl
from jax.experimental.pallas import tpu as pltpu
from jax.sharding import PartitionSpec as P

QHEADS = 64
KVHEADS = 8
HD = 128
PER = QHEADS // KVHEADS
SCALE = HD**-0.5 * 1.4426950408889634
FEW = 16
LIMIT = 1e30
NEG = -1e30
LANES = HD // 4
BLOCK = 2048
F32 = jnp.float32
BF16 = jnp.bfloat16


def dot_nt(a, b):
    return lax.dot_general(a, b, (((1,), (1,)), ((), ())), preferred_element_type=F32)


def dot_nn(a, b):
    return lax.dot_general(a, b, (((1,), (0,)), ((), ())), preferred_element_type=F32)


def dot_tn(a, b):
    return lax.dot_general(a, b, (((0,), (0,)), ((), ())), preferred_element_type=F32)


def split3(x):
    high = x.astype(BF16)
    rest = x - high.astype(F32)
    mid = rest.astype(BF16)
    return high, mid, (rest - mid.astype(F32)).astype(BF16)


def source_of(me, step):
    return me ^ step


def stacked(query, group):
    first = group * PER
    return jnp.concatenate([query[:, h * HD : (h + 1) * HD] for h in range(first, first + PER)], 0)


def turned_values(values, live):
    ones = jnp.ones((FEW, values.shape[0]), BF16)
    both = jnp.concatenate([values.T, ones], 0)
    if live is None:
        return both
    at = lax.broadcasted_iota(jnp.int32, both.shape, 1)
    return jnp.where(at < live, both, jnp.zeros_like(both))


def of_group(keys_ref, turned_ref, group, there):
    wide = keys_ref.shape[1]
    columns = slice(group * HD, (group + 1) * HD)
    turned = jnp.concatenate([turned_ref[columns, there], turned_ref[wide:, there]], 0)
    return keys_ref[there, columns], turned


def weighted(keys_ref, turned_ref, group, there, query, mark):
    keys, turned = of_group(keys_ref, turned_ref, group, there)
    weights = jnp.exp2(dot_nt(keys, query) * SCALE - mark * SCALE)
    return dot_nn(turned, weights.astype(BF16))


def blocks(tokens):
    size = min(BLOCK, tokens)
    return [slice(i, i + size) for i in range(0, tokens, size)]


def attend(query, keys_ref, turned_ref, acc, marks):
    for g in range(acc.shape[0]):
        q = stacked(query, g)
        mark = jnp.max(dot_nt(keys_ref[:FEW, g * HD : (g + 1) * HD], q), 0, keepdims=True)
        marks[g] = mark
        parts = [
            weighted(keys_ref, turned_ref, g, there, q, mark) for there in blocks(keys_ref.shape[0])
        ]
        acc[g] = functools.reduce(jnp.add, parts)


def overflowed(acc):
    return jnp.max(jnp.where(acc[:, HD : HD + 1, :] < LIMIT, 0.0, 1.0)) > 0.0


def again(query, keys_ref, turned_ref, acc, marks, length):
    block = min(256, keys_ref.shape[0])
    for g in range(acc.shape[0]):
        q = stacked(query, g)
        marks[g] = jnp.full(marks.shape[1:], NEG, F32)
        acc[g] = jnp.zeros(acc.shape[1:], F32)

        @pl.loop(0, (length + block - 1) // block)
        def _(i):
            keys, turned = of_group(
                keys_ref, turned_ref, g, pl.ds(pl.multiple_of(i * block, block), block)
            )
            scores = dot_nt(keys, q)
            valid = i * block + lax.broadcasted_iota(jnp.int32, scores.shape, 0) < length
            scores = jnp.where(valid, scores, NEG)
            old = marks[g]
            new = jnp.maximum(old, jnp.max(scores, 0, keepdims=True))
            weights = jnp.where(valid, jnp.exp2((scores - new) * SCALE), 0.0)
            acc[g] = acc[g] * jnp.exp2((old - new) * SCALE) + dot_nn(turned, weights.astype(BF16))
            marks[g] = new


def finish(acc, marks):
    groups = acc.shape[0]
    rows = acc.shape[2] // PER
    tiles, lines = [], []
    for g in range(groups):
        total = acc[g, HD : HD + 1, :]
        mean = (acc[g, :HD, :] * (1.0 / total)).T
        tiles += [mean[h * rows : (h + 1) * rows] for h in range(PER)]
        level = marks[g] * SCALE + jnp.log2(total)
        lines += [level[:, h * rows : (h + 1) * rows] for h in range(PER)]
    lines.append(jnp.full((HD - len(lines), rows), NEG, F32))
    return tiles, jnp.concatenate(lines, 0).T


def keep(result, mean_ref, level_ref):
    for head, mean in enumerate(result[0]):
        mean_ref[:, head * HD : (head + 1) * HD] = mean
    level_ref[...] = result[1]


def joined(tiles, level, spread, level_b):
    top = jnp.maximum(level, level_b)
    weight = jnp.exp2(level - top)
    weight_b = jnp.exp2(level_b - top)
    total = weight + weight_b
    share = weight / total
    share_b = weight_b / total
    tiles = [
        mean * share[:, head : head + 1]
        + spread[:, head * HD : (head + 1) * HD] * share_b[:, head : head + 1]
        for head, mean in enumerate(tiles)
    ]
    return tiles, top + jnp.log2(total)


def pack(tiles, level, out):
    for head, mean in enumerate(tiles):
        out[:, head * HD : (head + 1) * HD] = mean.astype(BF16)
    parts = [p[:, :LANES] for p in split3(level)]
    out[:, len(tiles) * HD :] = jnp.concatenate(parts + parts[:1], 1)


def prepare(
    count, axis, length_ref, owner_hbm, query_hbm, root_k_hbm, root_v_hbm, branch_k_hbm, branch_v_hbm,
    root_k, root_t, branch_k, branch_t, query_ref, picker_ref, owner_ref, root_v, branch_v, sems,
):
    local = query_ref.shape[0]
    rows = count * local
    slots = 2 * local
    copies = []

    def fetch(source, target):
        copies.append(pltpu.make_async_copy(source, target, sems.at[len(copies)]))
        return copies[-1]

    small = [fetch(owner_hbm, owner_ref), fetch(query_hbm, query_ref)]
    values = []
    for source, target, turned in ((root_v_hbm, root_v, root_t), (branch_v_hbm, branch_v, branch_t)):
        for there in parts_of(source.shape[0]):
            copy = fetch(source.at[pl.ds(there.start, there.stop - there.start), :], target.at[there, :])
            values.append((copy, target, turned, there))
    keys = [fetch(root_k_hbm, root_k), fetch(branch_k_hbm, branch_k)]
    for copy in copies:
        copy.start()

    me = lax.axis_index(axis)
    row = lax.broadcasted_iota(jnp.int32, (rows, rows), 0)
    column = lax.broadcasted_iota(jnp.int32, (rows, rows), 1)
    moved = source_of(me, column // local) * local + column % local == row
    small[0].wait()
    owner = owner_ref[...].reshape(1, rows).astype(F32)
    owner = dot_nn(jnp.broadcast_to(owner, (8, rows)).astype(BF16), moved.astype(F32).astype(BF16))
    member = owner[:1] == me.astype(F32)
    before = dot_nn(
        jnp.broadcast_to(member.astype(F32), (8, rows)).astype(BF16),
        (row < column).astype(F32).astype(BF16),
    )[:1]
    slot = lax.broadcasted_iota(jnp.int32, (slots, rows), 0).astype(F32)
    picker_ref[...] = jnp.where(member & (before == slot), 1.0, 0.0).astype(BF16)

    length = length_ref[0]
    for copy, source, turned, there in values:
        copy.wait()
        live = length - there.start if turned is branch_t else None
        turned[:, there] = turned_values(source[there, :], live)
    for copy in (small[1], *keys):
        copy.wait()


def parts_of(tokens):
    size = min(1024, tokens)
    return [slice(i, i + size) for i in range(0, tokens, size)]


def unit(first, second, root_k, root_t, mean_ref, level_ref, acc, marks):
    query = jnp.concatenate([first[...], second[...]], 0)
    attend(query, root_k, root_t, acc, marks)

    @pl.when(overflowed(acc))
    def _():
        again(query, root_k, root_t, acc, marks, root_k.shape[0])

    keep(finish(acc, marks), mean_ref, level_ref)


def main(count, *refs):
    length_ref, picker_ref, root_k, root_t, branch_k, branch_t = refs[:6]
    refs = refs[6:]
    queries, refs = refs[:count], refs[count:]
    more = max(0, count // 2 - 2)
    means, refs = refs[:more], refs[more:]
    levels, refs = refs[:more], refs[more:]
    outs, refs = refs[: count - 2], refs[count - 2 :]
    spread_ref, level_ref, root_acc, root_marks, branch_acc, branch_marks, mean_ref, mean_level = refs
    means = [mean_ref, *means]
    levels = [mean_level, *levels]
    local = queries[0].shape[0]
    length = length_ref[0]
    picker = picker_ref[...]
    pieces = [q[...] for q in queries]
    query = jnp.concatenate(pieces[2:4], 0)
    chosen = dot_nn(picker, jnp.concatenate(pieces, 0)).astype(BF16)
    attend(query, root_k, root_t, root_acc, root_marks)
    keep(finish(root_acc, root_marks), mean_ref, mean_level)
    attend(chosen, branch_k, branch_t, branch_acc, branch_marks)

    @pl.when(overflowed(root_acc) | overflowed(branch_acc))
    def _():
        again(query, root_k, root_t, root_acc, root_marks, root_k.shape[0])
        keep(finish(root_acc, root_marks), mean_ref, mean_level)
        again(chosen, branch_k, branch_t, branch_acc, branch_marks, length)

    tiles, level = finish(branch_acc, branch_marks)
    mixed = jnp.concatenate(tiles, 1)
    high = mixed.astype(BF16)
    low = (mixed - high.astype(F32)).astype(BF16)
    parts = split3(level)
    spread = dot_tn(picker, high) + dot_tn(picker, low)
    level_b = functools.reduce(jnp.add, [dot_tn(picker, part) for part in parts])
    held = dot_tn(picker, jnp.ones((2 * local, HD), BF16)) > 0.0
    level_b = jnp.where(held, level_b, NEG)
    spread_ref[...] = spread[: 2 * local]
    level_ref[...] = level_b[: 2 * local]
    for pair in range(1, count // 2):
        mean = means[pair - 1]
        tiles = [mean[:, i : i + HD] for i in range(0, mean.shape[1], HD)]
        level = levels[pair - 1][...]
        there = slice(2 * pair * local, 2 * (pair + 1) * local)
        tiles, level = joined(tiles, level, spread[there], level_b[there])
        for j in range(2):
            mine = slice(j * local, (j + 1) * local)
            pack([t[mine] for t in tiles], level[mine], outs[2 * (pair - 1) + j])


def local_pair(first, second, root_k, root_t, spread, level_b, mean_ref, level_ref, out, acc, marks):
    local = first.shape[0]
    query = jnp.concatenate([first[...], second[...]], 0)
    attend(query, root_k, root_t, acc, marks)

    @pl.when(overflowed(acc))
    def _():
        again(query, root_k, root_t, acc, marks, root_k.shape[0])

    tiles, level = finish(acc, marks)
    tiles, level = joined(tiles, level, spread[...], level_b[...])
    pack([t[local:] for t in tiles], level[local:], out)
    for head, mean in enumerate(tiles):
        mean_ref[:, head * HD : (head + 1) * HD] = mean[:local]
    level_ref[...] = level[:local]


def join(*refs):
    mean, level, out = refs[-3:]
    parts = refs[:-3]
    width = out.shape[1]
    levels = [level[:, :LANES]]
    for part in parts:
        aux = part[:, width:].astype(F32)
        levels.append(aux[:, :LANES] + aux[:, LANES : 2 * LANES] + aux[:, 2 * LANES : 3 * LANES])
    top = functools.reduce(jnp.maximum, levels)
    weights = [jnp.exp2(level - top) for level in levels]
    over = 1.0 / functools.reduce(jnp.add, weights)
    shares = [weight * over for weight in weights]
    for head in range(width // HD):
        tile = slice(head * HD, (head + 1) * HD)
        terms = [
            part[:, tile].astype(F32) * share[:, head : head + 1]
            for part, share in zip((mean, *parts), shares)
        ]
        out[:, tile] = functools.reduce(jnp.add, terms).astype(BF16)


def near(x):
    return pltpu.with_memory_space_constraint(x, pltpu.VMEM)


def call(kernel, name, outs, scratch, operands, smem=0, far=0, room=24, cost=None):
    vmem = pl.BlockSpec(memory_space=pltpu.VMEM)
    return pl.pallas_call(
        kernel,
        out_shape=[pltpu.VMEM(shape, dtype) for shape, dtype in outs],
        in_specs=[pl.BlockSpec(memory_space=pltpu.SMEM)] * smem
        + [pl.BlockSpec(memory_space=pltpu.HBM)] * far
        + [vmem] * (len(operands) - smem - far),
        out_specs=[vmem] * len(outs),
        scratch_shapes=scratch,
        compiler_params=pltpu.CompilerParams(vmem_limit_bytes=room * 2**20),
        cost_estimate=cost,
        name=name,
    )(
        *operands[:smem],
        *[pltpu.with_memory_space_constraint(x, pltpu.HBM) for x in operands[smem : smem + far]],
        *map(near, operands[smem + far :]),
    )


def on_device(
    axis, count, queries, root_keys, root_values, branch_keys, branch_values, branch_lengths, row_branch
):
    local, width = queries.shape
    tokens, wide = root_keys.shape
    kept = branch_keys.shape[1]
    pair = 2 * local
    columns = pair * PER
    sums = [
        pltpu.VMEM((wide // HD, HD + FEW, columns), F32),
        pltpu.VMEM((wide // HD, 1, columns), F32),
    ]
    message = ((local, width + HD), BF16)
    pair_form = [((pair, width), F32), ((pair, HD), F32)]

    def moved(x, step):
        return lax.ppermute(x, axis, [(source_of(i, step), i) for i in range(count)])

    got = {k: moved(queries, k) for k in [*range(2, count), 1]}
    root_k, root_t, branch_k, branch_t, own, picker = call(
        functools.partial(prepare, count, axis),
        "prepare",
        [
            ((tokens, wide), BF16),
            ((wide + FEW, tokens), BF16),
            ((kept, wide), BF16),
            ((wide + FEW, kept), BF16),
            ((local, width), BF16),
            ((pair, count * local), BF16),
        ],
        [
            pltpu.VMEM((count * local,), jnp.int32),
            pltpu.VMEM((tokens, wide), BF16),
            pltpu.VMEM((kept, wide), BF16),
            pltpu.SemaphoreType.DMA((4 + len(parts_of(tokens)) + len(parts_of(kept)),)),
        ],
        [
            branch_lengths,
            row_branch,
            queries,
            root_keys,
            root_values,
            branch_keys.reshape(branch_keys.shape[1:]),
            branch_values.reshape(branch_values.shape[1:]),
        ],
        smem=1,
        far=6,
    )
    got[0] = own
    units = [
        call(unit, "unit", pair_form, sums, [got[k], got[k + 1], root_k, root_t])
        for k in range(4, count, 2)
    ]
    *outs, spread, level_b = call(
        functools.partial(main, count),
        "main",
        [message] * (count - 2) + pair_form,
        sums + sums + [pltpu.VMEM(*shape) for shape in pair_form],
        [branch_lengths, picker, root_k, root_t, branch_k, branch_t]
        + [got[k] for k in range(count)]
        + [u[0] for u in units]
        + [u[1] for u in units],
        smem=1,
    )
    arrived = [moved(out, k) for k, out in enumerate(outs, 2)]
    mean, level, out = call(
        local_pair,
        "local_pair",
        [((local, width), F32), ((local, HD), F32), message],
        sums,
        [got[0], got[1], root_k, root_t, spread, level_b],
        cost=pl.CostEstimate(
            flops=4 * pair * tokens * width,
            transcendentals=pair * tokens * width // HD,
            bytes_accessed=4 * tokens * wide,
        ),
    )
    arrived.append(moved(out, 1))
    vmem = pl.BlockSpec(memory_space=pltpu.VMEM)
    return pl.pallas_call(
        join,
        out_shape=jax.ShapeDtypeStruct((local, width), BF16),
        in_specs=[vmem] * (1 + count),
        out_specs=vmem,
        compiler_params=pltpu.CompilerParams(vmem_limit_bytes=8 * 2**20),
        name="join",
    )(*map(near, [*arrived, mean, level]))


def solution(mesh):
    placed = (
        P(("groups", "branch"), "head"),
        P(("groups", "branch"), "head"),
        P(("groups", "branch"), "head"),
        P(("groups", "branch"), None, "head"),
        P(("groups", "branch"), None, "head"),
        P(("groups", "branch")),
        P("groups"),
    )
    return jax.shard_map(
        functools.partial(on_device, "branch", mesh.shape["branch"]),
        mesh=mesh,
        in_specs=placed,
        out_specs=P(("groups", "branch"), "head"),
        check_vma=False,
    )
```

```python
import functools

import jax
import jax.numpy as jnp
from jax import lax
from jax.experimental import pallas as pl
from jax.experimental.pallas import tpu as pltpu
from jax.sharding import PartitionSpec as P

QHEADS = 64
KVHEADS = 8
HD = 128
PER = QHEADS // KVHEADS
SCALE = HD**-0.5 * 1.4426950408889634
FEW = 16
LIMIT = 1e30
NEG = -1e30
LANES = HD // 4
BLOCK = 2048
F32 = jnp.float32
BF16 = jnp.bfloat16


def dot_nt(a, b):
    return lax.dot_general(a, b, (((1,), (1,)), ((), ())), preferred_element_type=F32)


def dot_nn(a, b):
    return lax.dot_general(a, b, (((1,), (0,)), ((), ())), preferred_element_type=F32)


def dot_tn(a, b):
    return lax.dot_general(a, b, (((0,), (0,)), ((), ())), preferred_element_type=F32)


def split3(x):
    high = x.astype(BF16)
    rest = x - high.astype(F32)
    mid = rest.astype(BF16)
    return high, mid, (rest - mid.astype(F32)).astype(BF16)


def source_of(me, step):
    return me ^ step


def stacked(query, group):
    first = group * PER
    return jnp.concatenate([query[:, h * HD : (h + 1) * HD] for h in range(first, first + PER)], 0)


def turned_values(values, live):
    ones = jnp.ones((FEW, values.shape[0]), BF16)
    both = jnp.concatenate([values.T, ones], 0)
    if live is None:
        return both
    at = lax.broadcasted_iota(jnp.int32, both.shape, 1)
    return jnp.where(at < live, both, jnp.zeros_like(both))


def of_group(keys_ref, turned_ref, group, there):
    wide = keys_ref.shape[1]
    columns = slice(group * HD, (group + 1) * HD)
    turned = jnp.concatenate([turned_ref[columns, there], turned_ref[wide:, there]], 0)
    return keys_ref[there, columns], turned


def weighted(keys_ref, turned_ref, group, there, query, mark):
    keys, turned = of_group(keys_ref, turned_ref, group, there)
    weights = jnp.exp2(dot_nt(keys, query) * SCALE - mark * SCALE)
    return dot_nn(turned, weights.astype(BF16))


def blocks(tokens):
    size = min(BLOCK, tokens)
    return [slice(i, i + size) for i in range(0, tokens, size)]


def attend(query, keys_ref, turned_ref, acc, marks):
    for g in range(acc.shape[0]):
        q = stacked(query, g)
        mark = jnp.max(dot_nt(keys_ref[:FEW, g * HD : (g + 1) * HD], q), 0, keepdims=True)
        marks[g] = mark
        parts = [
            weighted(keys_ref, turned_ref, g, there, q, mark) for there in blocks(keys_ref.shape[0])
        ]
        acc[g] = functools.reduce(jnp.add, parts)


def overflowed(acc):
    return jnp.max(jnp.where(acc[:, HD : HD + 1, :] < LIMIT, 0.0, 1.0)) > 0.0


def again(query, keys_ref, turned_ref, acc, marks, length):
    block = min(256, keys_ref.shape[0])
    for g in range(acc.shape[0]):
        q = stacked(query, g)
        marks[g] = jnp.full(marks.shape[1:], NEG, F32)
        acc[g] = jnp.zeros(acc.shape[1:], F32)

        @pl.loop(0, (length + block - 1) // block)
        def _(i):
            keys, turned = of_group(
                keys_ref, turned_ref, g, pl.ds(pl.multiple_of(i * block, block), block)
            )
            scores = dot_nt(keys, q)
            valid = i * block + lax.broadcasted_iota(jnp.int32, scores.shape, 0) < length
            scores = jnp.where(valid, scores, NEG)
            old = marks[g]
            new = jnp.maximum(old, jnp.max(scores, 0, keepdims=True))
            weights = jnp.where(valid, jnp.exp2((scores - new) * SCALE), 0.0)
            acc[g] = acc[g] * jnp.exp2((old - new) * SCALE) + dot_nn(turned, weights.astype(BF16))
            marks[g] = new


def finish(acc, marks):
    groups = acc.shape[0]
    rows = acc.shape[2] // PER
    tiles, lines = [], []
    for g in range(groups):
        total = acc[g, HD : HD + 1, :]
        mean = (acc[g, :HD, :] * (1.0 / total)).T
        tiles += [mean[h * rows : (h + 1) * rows] for h in range(PER)]
        level = marks[g] * SCALE + jnp.log2(total)
        lines += [level[:, h * rows : (h + 1) * rows] for h in range(PER)]
    lines.append(jnp.full((HD - len(lines), rows), NEG, F32))
    return tiles, jnp.concatenate(lines, 0).T


def keep(result, mean_ref, level_ref):
    for head, mean in enumerate(result[0]):
        mean_ref[:, head * HD : (head + 1) * HD] = mean
    level_ref[...] = result[1]


def joined(tiles, level, spread, level_b):
    top = jnp.maximum(level, level_b)
    weight = jnp.exp2(level - top)
    weight_b = jnp.exp2(level_b - top)
    total = weight + weight_b
    share = weight / total
    share_b = weight_b / total
    tiles = [
        mean * share[:, head : head + 1]
        + spread[:, head * HD : (head + 1) * HD] * share_b[:, head : head + 1]
        for head, mean in enumerate(tiles)
    ]
    return tiles, top + jnp.log2(total)


def pack(tiles, level, out):
    for head, mean in enumerate(tiles):
        out[:, head * HD : (head + 1) * HD] = mean.astype(BF16)
    parts = [p[:, :LANES] for p in split3(level)]
    out[:, len(tiles) * HD :] = jnp.concatenate(parts + parts[:1], 1)


def prepare(
    count, axis, length_ref, owner_hbm, query_hbm, root_k_hbm, root_v_hbm, branch_k_hbm, branch_v_hbm,
    root_k, root_t, branch_k, branch_t, query_ref, picker_ref, owner_ref, root_v, branch_v, sems,
):
    local = query_ref.shape[0]
    rows = count * local
    slots = 2 * local
    copies = []

    def fetch(source, target):
        copies.append(pltpu.make_async_copy(source, target, sems.at[len(copies)]))
        return copies[-1]

    small = [fetch(owner_hbm, owner_ref), fetch(query_hbm, query_ref)]
    values = []
    for source, target, turned in ((root_v_hbm, root_v, root_t), (branch_v_hbm, branch_v, branch_t)):
        for there in parts_of(source.shape[0]):
            copy = fetch(source.at[pl.ds(there.start, there.stop - there.start), :], target.at[there, :])
            values.append((copy, target, turned, there))
    keys = [fetch(root_k_hbm, root_k), fetch(branch_k_hbm, branch_k)]
    for copy in copies:
        copy.start()

    me = lax.axis_index(axis)
    row = lax.broadcasted_iota(jnp.int32, (rows, rows), 0)
    column = lax.broadcasted_iota(jnp.int32, (rows, rows), 1)
    moved = source_of(me, column // local) * local + column % local == row
    small[0].wait()
    owner = owner_ref[...].reshape(1, rows).astype(F32)
    owner = dot_nn(jnp.broadcast_to(owner, (8, rows)).astype(BF16), moved.astype(F32).astype(BF16))
    member = owner[:1] == me.astype(F32)
    before = dot_nn(
        jnp.broadcast_to(member.astype(F32), (8, rows)).astype(BF16),
        (row < column).astype(F32).astype(BF16),
    )[:1]
    slot = lax.broadcasted_iota(jnp.int32, (slots, rows), 0).astype(F32)
    picker_ref[...] = jnp.where(member & (before == slot), 1.0, 0.0).astype(BF16)

    length = length_ref[0]
    for copy, source, turned, there in values:
        copy.wait()
        live = length - there.start if turned is branch_t else None
        turned[:, there] = turned_values(source[there, :], live)
    for copy in (small[1], *keys):
        copy.wait()


def parts_of(tokens):
    size = min(1024, tokens)
    return [slice(i, i + size) for i in range(0, tokens, size)]


def unit(first, second, root_k, root_t, mean_ref, level_ref, acc, marks):
    query = jnp.concatenate([first[...], second[...]], 0)
    attend(query, root_k, root_t, acc, marks)

    @pl.when(overflowed(acc))
    def _():
        again(query, root_k, root_t, acc, marks, root_k.shape[0])

    keep(finish(acc, marks), mean_ref, level_ref)


def main(count, *refs):
    length_ref, picker_ref, root_k, root_t, branch_k, branch_t = refs[:6]
    refs = refs[6:]
    queries, refs = refs[:count], refs[count:]
    queries = (queries[-1], queries[-2], *queries[:-2])
    more = max(0, count // 2 - 2)
    means, refs = refs[:more], refs[more:]
    levels, refs = refs[:more], refs[more:]
    outs, refs = refs[: count - 2], refs[count - 2 :]
    spread_ref, level_ref, root_acc, root_marks, branch_acc, branch_marks, mean_ref, mean_level = refs
    means = [mean_ref, *means]
    levels = [mean_level, *levels]
    local = queries[0].shape[0]
    length = length_ref[0]
    picker = picker_ref[...]
    pieces = [q[...] for q in queries]
    query = jnp.concatenate(pieces[2:4], 0)
    chosen = dot_nn(picker, jnp.concatenate(pieces, 0)).astype(BF16)
    attend(query, root_k, root_t, root_acc, root_marks)
    keep(finish(root_acc, root_marks), mean_ref, mean_level)
    attend(chosen, branch_k, branch_t, branch_acc, branch_marks)

    @pl.when(overflowed(root_acc) | overflowed(branch_acc))
    def _():
        again(query, root_k, root_t, root_acc, root_marks, root_k.shape[0])
        keep(finish(root_acc, root_marks), mean_ref, mean_level)
        again(chosen, branch_k, branch_t, branch_acc, branch_marks, length)

    tiles, level = finish(branch_acc, branch_marks)
    mixed = jnp.concatenate(tiles, 1)
    high = mixed.astype(BF16)
    low = (mixed - high.astype(F32)).astype(BF16)
    parts = split3(level)
    spread = dot_tn(picker, high) + dot_tn(picker, low)
    level_b = functools.reduce(jnp.add, [dot_tn(picker, part) for part in parts])
    held = dot_tn(picker, jnp.ones((2 * local, HD), BF16)) > 0.0
    level_b = jnp.where(held, level_b, NEG)
    spread_ref[...] = spread[: 2 * local]
    level_ref[...] = level_b[: 2 * local]
    for pair in range(1, count // 2):
        mean = means[pair - 1]
        tiles = [mean[:, i : i + HD] for i in range(0, mean.shape[1], HD)]
        level = levels[pair - 1][...]
        there = slice(2 * pair * local, 2 * (pair + 1) * local)
        tiles, level = joined(tiles, level, spread[there], level_b[there])
        for j in range(2):
            mine = slice(j * local, (j + 1) * local)
            pack([t[mine] for t in tiles], level[mine], outs[2 * (pair - 1) + j])


def local_pair(first, second, root_k, root_t, spread, level_b, mean_ref, level_ref, out, acc, marks):
    local = first.shape[0]
    query = jnp.concatenate([first[...], second[...]], 0)
    attend(query, root_k, root_t, acc, marks)

    @pl.when(overflowed(acc))
    def _():
        again(query, root_k, root_t, acc, marks, root_k.shape[0])

    tiles, level = finish(acc, marks)
    tiles, level = joined(tiles, level, spread[...], level_b[...])
    pack([t[local:] for t in tiles], level[local:], out)
    for head, mean in enumerate(tiles):
        mean_ref[:, head * HD : (head + 1) * HD] = mean[:local]
    level_ref[...] = level[:local]


def join(*refs):
    mean, level, out = refs[-3:]
    parts = refs[:-3]
    width = out.shape[1]
    levels = [level[:, :LANES]]
    for part in parts:
        aux = part[:, width:].astype(F32)
        levels.append(aux[:, :LANES] + aux[:, LANES : 2 * LANES] + aux[:, 2 * LANES : 3 * LANES])
    top = functools.reduce(jnp.maximum, levels)
    weights = [jnp.exp2(level - top) for level in levels]
    over = 1.0 / functools.reduce(jnp.add, weights)
    shares = [weight * over for weight in weights]
    for head in range(width // HD):
        tile = slice(head * HD, (head + 1) * HD)
        terms = [
            part[:, tile].astype(F32) * share[:, head : head + 1]
            for part, share in zip((mean, *parts), shares)
        ]
        out[:, tile] = functools.reduce(jnp.add, terms).astype(BF16)


def near(x):
    return pltpu.with_memory_space_constraint(x, pltpu.VMEM)


def call(kernel, name, outs, scratch, operands, smem=0, far=0, room=24, cost=None):
    vmem = pl.BlockSpec(memory_space=pltpu.VMEM)
    return pl.pallas_call(
        kernel,
        out_shape=[pltpu.VMEM(shape, dtype) for shape, dtype in outs],
        in_specs=[pl.BlockSpec(memory_space=pltpu.SMEM)] * smem
        + [pl.BlockSpec(memory_space=pltpu.HBM)] * far
        + [vmem] * (len(operands) - smem - far),
        out_specs=[vmem] * len(outs),
        scratch_shapes=scratch,
        compiler_params=pltpu.CompilerParams(vmem_limit_bytes=room * 2**20),
        cost_estimate=cost,
        name=name,
    )(
        *operands[:smem],
        *[pltpu.with_memory_space_constraint(x, pltpu.HBM) for x in operands[smem : smem + far]],
        *map(near, operands[smem + far :]),
    )


def on_device(
    axis, count, queries, root_keys, root_values, branch_keys, branch_values, branch_lengths, row_branch
):
    local, width = queries.shape
    tokens, wide = root_keys.shape
    kept = branch_keys.shape[1]
    pair = 2 * local
    columns = pair * PER
    sums = [
        pltpu.VMEM((wide // HD, HD + FEW, columns), F32),
        pltpu.VMEM((wide // HD, 1, columns), F32),
    ]
    message = ((local, width + HD), BF16)
    pair_form = [((pair, width), F32), ((pair, HD), F32)]

    def moved(x, step):
        return lax.ppermute(x, axis, [(source_of(i, step), i) for i in range(count)])

    got = {k: moved(queries, k) for k in [*range(2, count), 1]}
    root_k, root_t, branch_k, branch_t, own, picker = call(
        functools.partial(prepare, count, axis),
        "prepare",
        [
            ((tokens, wide), BF16),
            ((wide + FEW, tokens), BF16),
            ((kept, wide), BF16),
            ((wide + FEW, kept), BF16),
            ((local, width), BF16),
            ((pair, count * local), BF16),
        ],
        [
            pltpu.VMEM((count * local,), jnp.int32),
            pltpu.VMEM((tokens, wide), BF16),
            pltpu.VMEM((kept, wide), BF16),
            pltpu.SemaphoreType.DMA((4 + len(parts_of(tokens)) + len(parts_of(kept)),)),
        ],
        [
            branch_lengths,
            row_branch,
            queries,
            root_keys,
            root_values,
            branch_keys.reshape(branch_keys.shape[1:]),
            branch_values.reshape(branch_values.shape[1:]),
        ],
        smem=1,
        far=6,
    )
    got[0] = own
    units = [
        call(unit, "unit", pair_form, sums, [got[k], got[k + 1], root_k, root_t])
        for k in range(4, count, 2)
    ]
    *outs, spread, level_b = call(
        functools.partial(main, count),
        "main",
        [message] * (count - 2) + pair_form,
        sums + sums + [pltpu.VMEM(*shape) for shape in pair_form],
        [branch_lengths, picker, root_k, root_t, branch_k, branch_t]
        + [got[k] for k in [*range(2, count), 1, 0]]
        + [u[0] for u in units]
        + [u[1] for u in units],
        smem=1,
    )
    arrived = [moved(out, k) for k, out in enumerate(outs, 2)]
    mean, level, out = call(
        local_pair,
        "local_pair",
        [((local, width), F32), ((local, HD), F32), message],
        sums,
        [got[0], got[1], root_k, root_t, spread, level_b],
        cost=pl.CostEstimate(
            flops=4 * pair * tokens * width,
            transcendentals=pair * tokens * width // HD,
            bytes_accessed=4 * tokens * wide,
        ),
    )
    arrived.append(moved(out, 1))
    vmem = pl.BlockSpec(memory_space=pltpu.VMEM)
    return pl.pallas_call(
        join,
        out_shape=jax.ShapeDtypeStruct((local, width), BF16),
        in_specs=[vmem] * (1 + count),
        out_specs=vmem,
        compiler_params=pltpu.CompilerParams(vmem_limit_bytes=8 * 2**20),
        name="join",
    )(*map(near, [*arrived, mean, level]))


def solution(mesh):
    placed = (
        P(("groups", "branch"), "head"),
        P(("groups", "branch"), "head"),
        P(("groups", "branch"), "head"),
        P(("groups", "branch"), None, "head"),
        P(("groups", "branch"), None, "head"),
        P(("groups", "branch")),
        P("groups"),
    )
    return jax.shard_map(
        functools.partial(on_device, "branch", mesh.shape["branch"]),
        mesh=mesh,
        in_specs=placed,
        out_specs=P(("groups", "branch"), "head"),
        check_vma=False,
    )
```
